32 devices in a mesh: groups: 2 (over x), gx: 16 (over z, y, core).
Axes of the slice: x: 2, y: 2, z: 4, core: 2. Of those that a mesh axis runs over, the one named last changes fastest.
Arguments:
- tokens: bfloat16 [4096, 1536], P(('groups', 'gx')), parts along dimension 0, may hold values from -6 to 6
- upstream: bfloat16 [4096, 1536], P(('groups', 'gx')), parts along dimension 0, may hold values from -6 to 6
- sample_of_token: int32 [4096], P(('groups', 'gx')), parts along dimension 0, may hold values from 0 to 15, never falling along the last dimension, each value on 1 to 256 neighbouring positions
- reward_level: int32 [32], P('groups'), parts along dimension 0, may hold values from 0 to 15
- up_weight: bfloat16 [6144, 1536], P('gx'), may hold values from -0.15625 to 0.15625
- down_weight: bfloat16 [6144, 1536], P('gx'), may hold values from -0.078125 to 0.078125
Outputs:
- grad_tokens: bfloat16 [4096, 1536], P(('groups', 'gx')), parts along dimension 0
- grad_up: float32 [12288, 1536], P(('groups', 'gx')), parts along dimension 0
- grad_down: float32 [12288, 1536], P(('groups', 'gx')), parts along dimension 0
The draws below stay inside these ranges and needn't reach their ends.
There are 2 independent parts, one for each index of `groups`. The reference program is written for one: setup_inputs(seed, part) draws one part's arguments, and reference() takes and returns one part's arrays. A program takes and returns all parts, laid end to end along the dimension named above; an argument that names none is the same for every part. Nothing has to cross between parts.
All inputs are finite; a program needn't handle non-finite values.
Results may differ from the reference program's by a relative error of at most 0.006.
Values may be sent and summed in bfloat16 or wider, within the bound.
No kernel may reach another device: no remote copies, remote signals or barrier semaphores. Data moves between devices by JAX's collectives and lax.ppermute only.
A program may use at most 128 MiB of HBM per device.

```python
import math
import jax
import jax.numpy as jnp
import numpy as np

D = 1536
FF = 6144
SAMPLES = 16
LEVELS = 16
TOKENS = 2048


def with_ends(result, own_key, least, largest):
    dims = result.shape
    index_at = [jax.random.randint(jax.random.fold_in(own_key, axis), (), 0, dims[axis]) for axis in range(len(dims))]
    result = result.at[tuple(index_at)].set(least)
    longest = dims.index(max(dims))
    index_at[longest] = (index_at[longest] + 1) % dims[longest]
    return result.at[tuple(index_at)].set(largest)


def shard_levels(stream_key, extent, pieces, least, largest):
    def one(axis_at, shards_of):
        steps = jax.random.uniform(jax.random.fold_in(jax.random.fold_in(stream_key, 6), axis_at), (shards_of,), jnp.float32, least / len(pieces), largest / len(pieces))
        return jnp.repeat(jnp.exp(steps), extent[axis_at] // shards_of).reshape((-1,) + (1,) * (len(extent) - axis_at - 1))

    loudness = one(*pieces[0])
    for cut in pieces[1:]:
        loudness = loudness * one(*cut)
    return loudness


def profile(number_of, total, bound, lean):
    weights = [(1 << 20) // math.isqrt(rank ** lean) + 1 for rank in range(2, number_of + 1)]
    rest, given = total - bound - (number_of - 1), [1] * (number_of - 1)
    while rest > 0:
        candidates = [i for i in range(number_of - 1) if given[i] < bound]
        mass, left = sum([weights[i] for i in candidates]), rest
        for i in candidates:
            extra = min(bound - given[i], max(1, left * weights[i] // mass), rest)
            given[i] = given[i] + extra
            rest = rest - extra
    return np.array([bound] + given)


def ragged_sizes(rng, amount, total, bound, lean):
    if amount == 2:
        one = jax.random.randint(rng, (), max(1, total - bound), min(bound, total - 1) + 1)
        return jnp.stack([one, total - one])
    sizes = jnp.asarray(profile(amount, total, bound, lean), jnp.int32)
    couples = (amount - 1) // 2
    donor, receiver = sizes[1:1 + 2 * couples:2], sizes[2:2 + 2 * couples:2]
    margin = jnp.minimum(donor - 1, bound - receiver)
    passed = jax.random.randint(jax.random.fold_in(rng, 1), (couples,), 0, 1 << 20) % (margin + 1)
    sizes = sizes.at[1:1 + 2 * couples:2].set(donor - passed).at[2:2 + 2 * couples:2].set(receiver + passed)
    return sizes[jax.random.permutation(jax.random.fold_in(rng, 2), amount)]


def gaussian(stream_key, dims, spread, most, shards=(), dtype=jnp.bfloat16):
    level = shard_levels(stream_key, dims, shards, -0.22, 0.18) if shards else 1.0
    drawn = jax.random.normal(stream_key, dims, jnp.float32) * spread * level
    return jnp.minimum(jnp.maximum(drawn, -most), most).astype(dtype)


def setup_inputs(seed: int = 0, part: int = 0) -> dict:
    key_of = jax.random.split(jax.random.key(seed), 7)
    part_keys = jax.random.split(jax.random.fold_in(key_of[6], part), 7)
    tokens = gaussian(part_keys[0], (TOKENS, D), 1.0, 6.0, ((0, 16),))
    upstream = gaussian(part_keys[1], (TOKENS, D), 1.0, 6.0, ((0, 16),))
    sample_of_token = jnp.searchsorted(jnp.cumsum(ragged_sizes(part_keys[2], SAMPLES, TOKENS, 2 * TOKENS // SAMPLES, 1)), jnp.arange(TOKENS), side="right").astype(jnp.int32)
    reward_level = with_ends(jax.random.randint(part_keys[3], (SAMPLES,), 0, LEVELS), jax.random.fold_in(part_keys[3], 1), 0, LEVELS - 1).astype(jnp.int32)
    up_weight = gaussian(key_of[4], (FF, D), D ** -0.5, 0.15625, ((0, 16),))
    down_weight = gaussian(key_of[5], (FF, D), FF ** -0.5, 0.078125, ((0, 16),))
    return {"tokens": tokens, "upstream": upstream, "sample_of_token": sample_of_token, "reward_level": reward_level, "up_weight": up_weight, "down_weight": down_weight}


def gelu_value(v):
    inner = 0.7978845608 * (v + 0.044715 * v * v * v)
    return 0.5 * v * (1.0 + jnp.tanh(inner))


def gelu_slope(v):
    inner = 0.7978845608 * (v + 0.044715 * v * v * v)
    hyper = jnp.tanh(inner)
    return 0.5 * (1.0 + hyper) + 0.5 * v * (1.0 - hyper * hyper) * 0.7978845608 * (1.0 + 3.0 * 0.044715 * v * v)


def reference(tokens, upstream, sample_of_token, reward_level, up_weight, down_weight):
    level = reward_level[sample_of_token]
    weight = (level + 1).astype(jnp.float32) / LEVELS
    weighted = (weight[:, None] * upstream.astype(jnp.float32)).astype(jnp.bfloat16)
    pre = jnp.dot(tokens, up_weight.T, preferred_element_type=jnp.float32)
    hidden = gelu_value(pre).astype(jnp.bfloat16)
    grad_hidden = jnp.dot(weighted, down_weight.T, preferred_element_type=jnp.float32)
    grad_pre = (grad_hidden * gelu_slope(pre)).astype(jnp.bfloat16)
    grad_down = jnp.dot(hidden.T, weighted, preferred_element_type=jnp.float32)
    grad_up = jnp.dot(grad_pre.T, tokens, preferred_element_type=jnp.float32)
    through = jnp.dot(grad_pre, up_weight, preferred_element_type=jnp.float32)
    grad_tokens = (weighted.astype(jnp.float32) + through).astype(jnp.bfloat16)
    return grad_tokens, grad_up, grad_down
```

```python
import jax
import jax.numpy as jnp
from jax import lax
from jax.sharding import PartitionSpec as P

LEVELS = 16
LAST = (((1,), (1,)), ((), ()))
FIRST = (((0,), (0,)), ((), ()))


def ring_order(chips):
    if chips <= 8:
        return list(range(0, chips, 2)) + list(range(1, chips, 2))[::-1]
    return list(range(chips))


def ring_route(count):
    order = ring_order(count // 2)
    chips = len(order)
    route = []
    for place in range(chips):
        here = order[place]
        route.append((2 * here, 2 * order[(place + 1) % chips]))
        route.append((2 * here + 1, 2 * order[(place - 1) % chips] + 1))
    return route


def gelu_pair(v):
    inner = 0.7978845608 * (v + 0.044715 * v * v * v)
    hyper = jnp.tanh(inner)
    value = 0.5 * v * (1.0 + hyper)
    slope = 0.5 * (1.0 + hyper) + 0.5 * v * (1.0 - hyper * hyper) * 0.7978845608 * (
        1.0 + 3.0 * 0.044715 * v * v
    )
    return value, slope


def dot(a, b, dims):
    return lax.dot_general(a, b, dims, preferred_element_type=jnp.float32)


def local(tokens, upstream, sample_of_token, reward_level, up_weight, down_weight):
    count = lax.axis_size("gx")
    chips = count // 2
    route = ring_route(count)
    swap = [(i, i ^ 1) for i in range(count)]

    def hop(block):
        return lax.ppermute(block, "gx", route)

    def across(block):
        return lax.ppermute(block, "gx", swap)

    matches = sample_of_token[:, None] == jnp.arange(reward_level.shape[0], dtype=jnp.int32)[None, :]
    level = jnp.sum(jnp.where(matches, reward_level[None, :], 0), axis=1)
    weight = (level + 1).astype(jnp.float32) / LEVELS
    weighted = (weight[:, None] * upstream.astype(jnp.float32)).astype(jnp.bfloat16)

    units = up_weight.shape[0]
    up_rows = jnp.concatenate([up_weight, across(up_weight)], axis=0)
    down_rows = jnp.concatenate([down_weight, across(down_weight)], axis=0)

    x, g = tokens, weighted
    xs, gs, hs, ps = [], [], [], []
    carried = None
    own_part = None
    for step in range(chips):
        if step:
            x, g = hop(x), hop(g)
        pre = dot(x, up_rows, LAST)
        value, slope = gelu_pair(pre)
        hidden = value.astype(jnp.bfloat16)
        grad_pre = (dot(g, down_rows, LAST) * slope).astype(jnp.bfloat16)
        xs.append(x)
        gs.append(g)
        hs.append(hidden)
        ps.append(grad_pre)
        part = dot(grad_pre, up_rows, (((1,), (0,)), ((), ())))
        if step == 0:
            own_part = part
        else:
            total = part if carried is None else part + carried.astype(jnp.float32)
            carried = hop(total.astype(jnp.bfloat16))
    grad_tokens = (
        weighted.astype(jnp.float32) + own_part + carried.astype(jnp.float32)
    ).astype(jnp.bfloat16)

    x_all, g_all = jnp.concatenate(xs), jnp.concatenate(gs)
    h_all, p_all = jnp.concatenate(hs), jnp.concatenate(ps)
    up_other = across(dot(p_all[:, units:], x_all, FIRST).astype(jnp.bfloat16))
    down_other = across(dot(h_all[:, units:], g_all, FIRST).astype(jnp.bfloat16))
    grad_up = dot(p_all[:, :units], x_all, FIRST) + up_other.astype(jnp.float32)
    grad_down = dot(h_all[:, :units], g_all, FIRST) + down_other.astype(jnp.float32)
    return grad_tokens, grad_up, grad_down


def solution(mesh):
    rows = P(("groups", "gx"), None)
    return jax.shard_map(
        local,
        mesh=mesh,
        in_specs=(rows, rows, P(("groups", "gx")), P("groups"), P("gx", None), P("gx", None)),
        out_specs=(rows, rows, rows),
        check_vma=False,
    )
```

```python
import jax
import jax.numpy as jnp
from jax import lax
from jax.sharding import PartitionSpec as P

LEVELS = 16
LAST = (((1,), (1,)), ((), ()))
ROWS = (((1,), (0,)), ((), ()))
FIRST = (((0,), (0,)), ((), ()))


def ring_order(chips):
    if chips <= 8:
        return list(range(0, chips, 2)) + list(range(1, chips, 2))[::-1]
    return list(range(chips))


def ring_route(count):
    order = ring_order(count // 2)
    chips = len(order)
    route = []
    for place in range(chips):
        here = order[place]
        route.append((2 * here, 2 * order[(place + 1) % chips]))
        route.append((2 * here + 1, 2 * order[(place - 1) % chips] + 1))
    return route


def gelu_pair(v):
    inner = 0.7978845608 * (v + 0.044715 * v * v * v)
    hyper = jnp.tanh(inner)
    value = 0.5 * v * (1.0 + hyper)
    slope = 0.5 * (1.0 + hyper) + 0.5 * v * (1.0 - hyper * hyper) * 0.7978845608 * (
        1.0 + 3.0 * 0.044715 * v * v
    )
    return value, slope


def dot(a, b, dims):
    return lax.dot_general(a, b, dims, preferred_element_type=jnp.float32)


def behind(block, *earlier):
    return lax.optimization_barrier((block, earlier))[0]


def local(tokens, upstream, sample_of_token, reward_level, up_weight, down_weight):
    count = lax.axis_size("gx")
    chips = count // 2
    route = ring_route(count)
    swap = [(i, i ^ 1) for i in range(count)]

    def hop(block, name):
        with jax.named_scope(name):
            return lax.ppermute(block, "gx", route)

    def across(block, name):
        with jax.named_scope(name):
            return lax.ppermute(block, "gx", swap)

    x_next = hop(tokens, "hop_x")
    matches = sample_of_token[:, None] == jnp.arange(reward_level.shape[0], dtype=jnp.int32)[None, :]
    level = jnp.sum(jnp.where(matches, reward_level[None, :], 0), axis=1)
    weight = (level + 1).astype(jnp.float32) / LEVELS
    weighted = (weight[:, None] * behind(upstream, tokens, up_weight).astype(jnp.float32)).astype(jnp.bfloat16)
    g_next = hop(weighted, "hop_g")


    units = up_weight.shape[0]
    own, other = slice(0, units), slice(units, None)
    up_rows = jnp.concatenate([up_weight, across(up_weight, "swap_up")], axis=0)
    down_rows = jnp.concatenate([down_weight, across(down_weight, "swap_down")], axis=0)

    def middle(x, g):
        value, slope = gelu_pair(dot(x, up_rows, LAST))
        hidden = value.astype(jnp.bfloat16)
        return x, g, hidden, (dot(g, down_rows, LAST) * slope).astype(jnp.bfloat16)

    def gradients(waiting, side):
        x, g, hidden, grad_pre = [jnp.concatenate(blocks) for blocks in zip(*waiting)]
        return [dot(grad_pre[:, side], x, FIRST), dot(hidden[:, side], g, FIRST)]

    def add(sums, more):
        return more if sums is None else [a + b for a, b in zip(sums, more)]

    due = []
    waiting, mine, theirs, carried, base = [], None, None, None, None
    for step in range(1, chips):
        x, g = x_next, g_next
        if step == 1:
            g = behind(g, dot(x, up_rows, LAST))
        if step < chips - 1:
            x_next, g_next = hop(x, "hop_x"), hop(g, "hop_g")
        waiting.append(middle(x, g))
        if step == chips - 1:
            with jax.named_scope("last"):
                mine = add(mine, gradients(waiting, own))
                theirs = [a.astype(jnp.bfloat16) for a in add(theirs, gradients(waiting, other))]
            carried = behind(carried, waiting[-1], theirs)
        with jax.named_scope("token_part"):
            total = dot(waiting[-1][3], up_rows, ROWS)
            if carried is not None:
                total = total + carried.astype(jnp.float32)
            total = total.astype(jnp.bfloat16)
        arrived = carried
        carried = hop(total, "hop_sum")
        done = [total]
        if step == 1:
            waiting.append(middle(behind(tokens, total), weighted))
            base = weighted.astype(jnp.float32) + dot(waiting[-1][3], up_rows, ROWS)
        elif step == 2:
            done.append(base)
        done += due
        if step in (chips // 2, chips - 3):
            with jax.named_scope("batch"):
                waiting = [behind(blocks, total) for blocks in waiting]
                mine = add(mine, gradients(waiting, own))
                theirs = add(theirs, gradients(waiting, other))
            waiting = []
            due = mine + theirs
        if step < chips - 1:
            x_next, g_next = behind(x_next, *done), behind(g_next, *done)

    received = [across(behind(a, arrived), "swap_grads") for a in theirs]
    with jax.named_scope("finish"):
        grad_up, grad_down = [a + b.astype(jnp.float32) for a, b in zip(mine, received)]
        carried, grad_up, grad_down = lax.optimization_barrier((carried, grad_up, grad_down))
        grad_tokens = (base + carried.astype(jnp.float32)).astype(jnp.bfloat16)
    return grad_tokens, grad_up, grad_down


def solution(mesh):
    rows = P(("groups", "gx"), None)
    return jax.shard_map(
        local,
        mesh=mesh,
        in_specs=(rows, rows, P(("groups", "gx")), P("groups"), P("gx", None), P("gx", None)),
        out_specs=(rows, rows, rows),
        check_vma=False,
    )
```

```python
import jax
import jax.numpy as jnp
from jax import lax
from jax.sharding import PartitionSpec as P

LEVELS = 16
LAST = (((1,), (1,)), ((), ()))
ROWS = (((1,), (0,)), ((), ()))
FIRST = (((0,), (0,)), ((), ()))


def ring_order(chips):
    if chips <= 8:
        return list(range(0, chips, 2)) + list(range(1, chips, 2))[::-1]
    return list(range(chips))


def ring_route(count):
    order = ring_order(count // 2)
    chips = len(order)
    route = []
    for place in range(chips):
        here = order[place]
        route.append((2 * here, 2 * order[(place + 1) % chips]))
        route.append((2 * here + 1, 2 * order[(place - 1) % chips] + 1))
    return route


def gelu_pair(v):
    inner = 0.7978845608 * (v + 0.044715 * v * v * v)
    hyper = jnp.tanh(inner)
    value = 0.5 * v * (1.0 + hyper)
    slope = 0.5 * (1.0 + hyper) + 0.5 * v * (1.0 - hyper * hyper) * 0.7978845608 * (
        1.0 + 3.0 * 0.044715 * v * v
    )
    return value, slope


def dot(a, b, dims):
    return lax.dot_general(a, b, dims, preferred_element_type=jnp.float32)


def behind(block, *earlier):
    return lax.optimization_barrier((block, earlier))[0]


def local(tokens, upstream, sample_of_token, reward_level, up_weight, down_weight):
    count = lax.axis_size("gx")
    chips = count // 2
    route = ring_route(count)
    swap = [(i, i ^ 1) for i in range(count)]

    def hop(block, name):
        with jax.named_scope(name):
            return lax.ppermute(block, "gx", route)

    def across(block, name):
        with jax.named_scope(name):
            return lax.ppermute(block, "gx", swap)

    x_next = hop(tokens, "hop_x")
    matches = sample_of_token[:, None] == jnp.arange(reward_level.shape[0], dtype=jnp.int32)[None, :]
    level = jnp.sum(jnp.where(matches, reward_level[None, :], 0), axis=1)
    weight = (level + 1).astype(jnp.float32) / LEVELS
    weighted = (weight[:, None] * behind(upstream, tokens, up_weight).astype(jnp.float32)).astype(jnp.bfloat16)
    g_next = hop(weighted, "hop_g")


    units = up_weight.shape[0]
    own, other = slice(0, units), slice(units, None)
    up_rows = jnp.concatenate([up_weight, across(up_weight, "swap_up")], axis=0)
    down_rows = jnp.concatenate([down_weight, across(down_weight, "swap_down")], axis=0)

    width = up_rows.shape[1]
    span = width // 2
    starts = range(0, width, span)
    up_cuts = [up_rows[:, at:at + span] for at in starts]

    def middle(x, g):
        value, slope = gelu_pair(dot(x, up_rows, LAST))
        hidden = value.astype(jnp.bfloat16)
        return x, g, hidden, (dot(g, down_rows, LAST) * slope).astype(jnp.bfloat16)

    def gradients(waiting, side):
        x, g, hidden, grad_pre = [jnp.concatenate(blocks) for blocks in zip(*waiting)]
        return [dot(grad_pre[:, side], x, FIRST), dot(hidden[:, side], g, FIRST)]

    def add(sums, more):
        return more if sums is None else [a + b for a, b in zip(sums, more)]

    due = []
    waiting, mine, theirs, carried, base = [], None, None, None, None
    for step in range(1, chips):
        x, g = x_next, g_next
        if step == 1:
            g = behind(g, dot(x, up_rows, LAST))
        if step < chips - 1:
            x_next, g_next = hop(x, "hop_x"), hop(g, "hop_g")
        waiting.append(middle(x, g))
        if step == chips - 1:
            with jax.named_scope("last"):
                mine = add(mine, gradients(waiting, own))
                theirs = [a.astype(jnp.bfloat16) for a in add(theirs, gradients(waiting, other))]
            carried = [behind(part, waiting[-1], theirs) for part in carried]
        with jax.named_scope("token_part"):
            if step < chips - 2:
                totals = [dot(waiting[-1][3], up_rows, ROWS)]
            else:
                totals = [dot(waiting[-1][3], columns, ROWS) for columns in up_cuts]
            if step == chips - 2:
                carried = [carried[0][:, at:at + span] for at in starts]
            if carried is not None:
                totals = [a + b.astype(jnp.float32) for a, b in zip(totals, carried)]
            totals = [a.astype(jnp.bfloat16) for a in totals]
        arrived = carried
        if step == chips - 1:
            pass
        carried = [hop(total, "hop_sum") for total in totals]
        total = totals[0]
        done = list(totals)
        if step == 1:
            waiting.append(middle(behind(tokens, total), weighted))
            base = weighted.astype(jnp.float32) + dot(waiting[-1][3], up_rows, ROWS)
        elif step == 2:
            done.append(base)
        done += due
        if step in (chips // 2, chips - 3):
            with jax.named_scope("batch"):
                waiting = [behind(blocks, total) for blocks in waiting]
                mine = add(mine, gradients(waiting, own))
                theirs = add(theirs, gradients(waiting, other))
            waiting = []
            due = mine + theirs
        if step < chips - 1:
            x_next, g_next = behind(x_next, *done), behind(g_next, *done)

    received = [across(behind(a, arrived[0]), "swap_grads") for a in theirs]
    with jax.named_scope("finish"):
        mine = [behind(a, carried[0]) for a in mine]
        grad_up, grad_down = [a + b.astype(jnp.float32) for a, b in zip(mine, received)]
        carried, grad_up, grad_down = lax.optimization_barrier((carried, grad_up, grad_down))
        grad_tokens = jnp.concatenate(
            [
                (base[:, at:at + span] + part.astype(jnp.float32)).astype(jnp.bfloat16)
                for at, part in zip(starts, carried)
            ],
            axis=1,
        )
    return grad_tokens, grad_up, grad_down


def solution(mesh):
    rows = P(("groups", "gx"), None)
    return jax.shard_map(
        local,
        mesh=mesh,
        in_specs=(rows, rows, P(("groups", "gx")), P("groups"), P("gx", None), P("gx", None)),
        out_specs=(rows, rows, rows),
        check_vma=False,
    )
```
